32 devices in a mesh: gx: 4 (over z), gy: 2 (over y), gz: 4 (over x, core).
Axes of the slice: x: 2, y: 2, z: 4, core: 2. Of those that a mesh axis runs over, the one named last changes fastest.
Arguments:
- velocity: float32 [3, 32, 16, 512], P(None, 'gx', 'gy', 'gz'), may hold values from -4 to 4
- sketch_prev: float32 [3, 16, 4, 32, 8, 128], P(None, 'gy', 'gz', 'gx'), may hold values from -6 to 6
- seed_matrix: int32 [512, 128], replicated, may hold values from -4 to 4
- snap_steps: int32 [4], replicated, may hold values from 0 to 511
- rank_keep: int32 [1], replicated, may hold values from 32 to 128
Outputs:
- velocity_out: float32 [3, 32, 16, 512], P(None, 'gx', 'gy', 'gz')
- mode_rows: float32 [3, 16, 4, 32, 8, 128], P(None, 'gy', 'gz', 'gx')
- factor: float32 [128, 128], replicated
The draws below stay inside these ranges and needn't reach their ends.
All inputs are finite; a program needn't handle non-finite values.
Results may differ from the reference program's by a relative error of at most 0.0003.
Values sent between devices are 32-bit elements; how exact they have to be, the bound alone decides.
A program may use at most 64 MiB of HBM per device.

```python
import math
import jax
import jax.numpy as jnp
from jax import lax

SNAPS = 4
STEPS = 2
R = 128
MTOT = 512
NX = 32
NY = 16
NZ = 512
XC = 8
ZC = 128
ZCD = 32
NROWS = 49152
N_GZ = 4


def draw_sketch_prev(key, part):
    subkeys = jax.random.split(key, 4)
    full_shape = (3, NY, N_GZ, ZCD, XC, R)
    wall_frac = jnp.arange(NY, dtype=jnp.float32).reshape(1, NY, 1, 1, 1, 1) / max(NY - 1, 1)
    span_cells = jnp.arange(N_GZ, dtype=jnp.float32).reshape(1, 1, N_GZ, 1, 1, 1) * ZCD + jnp.arange(ZCD, dtype=jnp.float32).reshape(1, 1, 1, ZCD, 1, 1)
    span_frac = span_cells / max(N_GZ * ZCD - 1, 1)
    ramp_up = 1.0 + wall_frac + span_frac
    row_scale = jnp.exp(jax.random.uniform(subkeys[0], (3, NY, N_GZ, ZCD, XC, 1), jnp.float32) * math.log(10.0))
    noise = jax.random.truncated_normal(subkeys[1], -4.0, 4.0, full_shape, jnp.float32)
    col_scale = jnp.exp(jax.random.uniform(subkeys[3], (R,), jnp.float32) * math.log(10.0))
    return jnp.clip(0.02 * noise * row_scale * col_scale * ramp_up, -6.0, 6.0)


def plant(entries, rng, low, largest):
    longest = entries.shape.index(max(entries.shape))
    spots = []
    for shift in (0, 1):
        where = [jax.random.randint(jax.random.fold_in(rng, axis), (), 0, length) for axis, length in enumerate(entries.shape)]
        where[longest] = (where[longest] + shift) % entries.shape[longest]
        spots.append(tuple(where))
    return entries.at[spots[0]].set(low).at[spots[1]].set(largest)


def levels(rng, extent, shards, least, top_value):
    factor_of, own = 1.0, jax.random.fold_in(rng, 6)
    for position, parts in shards:
        heights = jnp.exp(jax.random.uniform(jax.random.fold_in(own, position), (parts,), jnp.float32, least / len(shards), top_value / len(shards)))
        factor_of = factor_of * jnp.repeat(heights, extent[position] // parts).reshape([-1 if axis == position else 1 for axis in range(len(extent))])
    return factor_of


def scatter_about(rng, dims, scale, most, pieces=(), kind=jnp.bfloat16):
    factor_of = levels(rng, dims, pieces, -0.22, 0.18) if pieces else 1.0
    values = jax.random.normal(rng, dims, jnp.float32) * scale * factor_of
    return jnp.minimum(jnp.maximum(values, -most), most).astype(kind)


def setup_inputs(seed: int = 0) -> dict:
    key_list = jax.random.split(jax.random.key(seed), 6)
    velocity = scatter_about(key_list[0], (3, NX, NY, NZ), 1.0, 4.0, ((1, 4), (2, 2), (3, 4)), jnp.float32)
    sketch_prev = draw_sketch_prev(jax.random.fold_in(key_list[5], 71), 0)
    seed_matrix = plant(jax.random.randint(key_list[2], (MTOT, R), -4, 5), jax.random.fold_in(key_list[2], 1), -4, 4).astype(jnp.int32)
    snap_steps = plant(jax.random.randint(key_list[3], (SNAPS,), 0, MTOT), jax.random.fold_in(key_list[3], 1), 0, MTOT - 1).astype(jnp.int32)
    rank_keep = jax.random.randint(key_list[4], (1,), R // 4, R + 1).astype(jnp.int32)
    return {"velocity": velocity, "sketch_prev": sketch_prev, "seed_matrix": seed_matrix, "snap_steps": snap_steps, "rank_keep": rank_keep}


TIME_STEP = 0.1
VISCOSITY = 0.4
ONE_THIRD = 1.0 / 3.0
TWO_THIRDS = 2.0 / 3.0
HIGHEST = lax.Precision.HIGHEST

def tendency(padded):
    center = padded[:, 1:-1, 1:-1, 1:-1]
    forward = (padded[:, 2:, 1:-1, 1:-1], padded[:, 1:-1, 2:, 1:-1], padded[:, 1:-1, 1:-1, 2:])
    backward = (padded[:, :-2, 1:-1, 1:-1], padded[:, 1:-1, :-2, 1:-1], padded[:, 1:-1, 1:-1, :-2])
    convect = center[0:1] * (forward[0] - backward[0]) + center[1:2] * (forward[1] - backward[1]) + center[2:3] * (forward[2] - backward[2])
    spread = forward[0] + backward[0] + forward[1] + backward[1] + forward[2] + backward[2] - 6.0 * center
    return -0.5 * convect + VISCOSITY * spread

def pad_walls(current):
    wrapped = jnp.pad(current, ((0, 0), (1, 1), (0, 0), (1, 1)), mode='wrap')
    return jnp.pad(wrapped, ((0, 0), (0, 0), (1, 1), (0, 0)))

def runge_step(current):
    first_section = current + TIME_STEP * tendency(pad_walls(current))
    second_section = 0.75 * current + 0.25 * (first_section + TIME_STEP * tendency(pad_walls(first_section)))
    return ONE_THIRD * current + TWO_THIRDS * (second_section + TIME_STEP * tendency(pad_walls(second_section)))

def reference(velocity, sketch_prev, seed_matrix, snap_steps, rank_keep):
    current = velocity
    snapshots = []
    for snap_index in range(SNAPS):
        for step_index in range(STEPS):
            current = runge_step(current)
        blocks = current.reshape(3, XC, 4, NY, ZC, 4)
        coarse = jnp.transpose(lax.optimization_barrier(jnp.mean(blocks, axis=(2, 5))), (0, 2, 3, 1))
        snapshots.append(coarse.reshape(-1))
    stacked = jnp.stack(snapshots)
    picker = (snap_steps[:, None] == jnp.arange(MTOT, dtype=jnp.int32)[None, :]).astype(jnp.float32)
    omega_rows = 0.5 * jnp.dot(picker, seed_matrix.astype(jnp.float32), precision=HIGHEST)
    sketch_rows = sketch_prev.reshape(-1, R) + lax.dot_general(stacked, omega_rows, (((0,), (0,)), ((), ())), precision=HIGHEST)
    gram_sum = lax.dot_general(sketch_rows, sketch_rows, (((0,), (0,)), ((), ())), precision=HIGHEST)
    lower_factor = jnp.linalg.cholesky(gram_sum)
    identity = jnp.eye(R, dtype=jnp.float32)
    inverse = lax.linalg.triangular_solve(lower_factor, identity, left_side=True, lower=True).T
    norm_scale = math.sqrt(NROWS)
    inside = (jnp.arange(R, dtype=jnp.int32) < rank_keep[0]).astype(jnp.float32)
    mode_rows = norm_scale * jnp.dot(sketch_rows, inverse, precision=HIGHEST) * inside[None, :]
    factor = lower_factor.T * (1.0 / norm_scale) * inside[:, None] * inside[None, :]
    return (current, mode_rows.reshape(3, NY, N_GZ, ZCD, XC, R), factor)
```

```python
import functools
import math

import jax
import jax.numpy as jnp
from jax import lax
from jax.experimental import pallas as pl
from jax.experimental.pallas import tpu as pltpu
from jax.sharding import PartitionSpec as P

MESH = pl.DeviceIdType.MESH
VMEM_SPEC = pl.BlockSpec(memory_space=pltpu.VMEM)

SNAPS = 4
STEPS = 2


TIME_STEP = 0.1
VISCOSITY = 0.4
ONE_THIRD = 1.0 / 3.0
TWO_THIRDS = 2.0 / 3.0
HIGHEST = lax.Precision.HIGHEST


def extended(block, sides, width):
    for axis, dim in sides:
        count = lax.axis_size(axis)
        forward = [(i, i + 1) for i in range(count - 1)]
        forward.append((count - 1, 0))
        backward = [(target, source) for source, target in forward]
        low = lax.ppermute(
            lax.slice_in_dim(block, block.shape[dim] - width, None, axis=dim), axis, forward
        )
        high = lax.ppermute(lax.slice_in_dim(block, 0, width, axis=dim), axis, backward)
        block = jnp.concatenate([low, block, high], axis=dim)
    return block


def tendency(padded):
    center = padded[:, 1:-1, 1:-1, 1:-1]
    forward = (padded[:, 2:, 1:-1, 1:-1], padded[:, 1:-1, 2:, 1:-1], padded[:, 1:-1, 1:-1, 2:])
    backward = (padded[:, :-2, 1:-1, 1:-1], padded[:, 1:-1, :-2, 1:-1], padded[:, 1:-1, 1:-1, :-2])
    convect = (
        center[0:1] * (forward[0] - backward[0])
        + center[1:2] * (forward[1] - backward[1])
        + center[2:3] * (forward[2] - backward[2])
    )
    spread = (
        forward[0]
        + backward[0]
        + forward[1]
        + backward[1]
        + forward[2]
        + backward[2]
        - 6.0 * center
    )
    return -0.5 * convect + VISCOSITY * spread


def with_walls(padded, margin):
    cells_y = padded.shape[2] - 2 * margin
    wall_rows = (
        lax.axis_index("gy") * cells_y - margin + jnp.arange(cells_y + 2 * margin, dtype=jnp.int32)
    )
    inside = ((wall_rows >= 0) & (wall_rows < lax.axis_size("gy") * cells_y)).astype(jnp.float32)
    return padded * inside[None, None, :, None]


def faces_padded(current):
    return with_walls(extended(current, (("gx", 1), ("gy", 2), ("gz", 3)), 1), 1)


def step_by_section(current):
    first_section = current + TIME_STEP * tendency(faces_padded(current))
    second_section = 0.75 * current + 0.25 * (
        first_section + TIME_STEP * tendency(faces_padded(first_section))
    )
    return ONE_THIRD * current + TWO_THIRDS * (
        second_section + TIME_STEP * tendency(faces_padded(second_section))
    )


def coarse_local(current):
    cells_x = current.shape[1]
    cells_y = current.shape[2]
    cells_z = current.shape[3]
    blocks = current.reshape(3, cells_x // 4, 4, cells_y, cells_z // 4, 4)
    return jnp.transpose(jnp.mean(blocks, axis=(2, 5)), (0, 2, 3, 1))


GROUP = 8
CHUNK = 16
HALO = 24
REACH = (-2, -1, 0, 1, 2)


def place_of(n):
    m = n % GROUP
    return (m // 2, m % 2, n // GROUP)


def swap_groups(rows):
    rows = list(rows)
    lane = lax.broadcasted_iota(jnp.int32, rows[0].shape, 1)
    for step in (1, 2, 4):
        low = (lane // (CHUNK * step)) % 2 == 0
        for i in range(GROUP):
            if i & step:
                continue
            first, second = rows[i], rows[i | step]
            rows[i] = jnp.where(low, first, pltpu.roll(second, CHUNK * step, 1))
            rows[i | step] = jnp.where(low, pltpu.roll(first, 128 - CHUNK * step, 1), second)
    return rows


def meet(places):
    barrier = pltpu.get_barrier_semaphore()
    for place in places:
        pl.semaphore_signal(barrier, inc=1, device_id=place, device_id_type=MESH)
    pl.semaphore_wait(barrier, len(places))


def gather_kernel(ring, v_ref, ext_ref, packed, send_a, recv_a, send_b, recv_b):
    gx, gy, gz = lax.axis_index("gx"), lax.axis_index("gy"), lax.axis_index("gz")
    m = 2 * gx + gy
    n = GROUP * gz + m
    mates = [((m + j) % GROUP) for j in range(1, GROUP)]
    mate_places = [(k // 2, k % 2, gz) for k in mates]
    offsets = [d for d in REACH if d != 0]
    ring_places = [place_of((n + d + ring) % ring) for d in offsets]
    rows = swap_groups([v_ref[:, x].reshape(24, 128) for x in range(8)])
    for k in range(GROUP):
        packed[k] = rows[k].reshape(3, 8, 128)
    meet(mate_places + ring_places)
    copies = []
    for j in range(1, GROUP):
        copy = pltpu.make_async_remote_copy(
            src_ref=packed.at[mates[j - 1]],
            dst_ref=ext_ref.at[2, m],
            send_sem=send_a.at[j - 1],
            recv_sem=recv_a.at[j - 1],
            device_id=mate_places[j - 1],
            device_id_type=MESH,
        )
        copy.start()
        copies.append(copy)
    ext_ref[2, m] = packed[m]
    for copy in copies:
        copy.wait()
    copies = []
    for i, d in enumerate(offsets):
        copy = pltpu.make_async_remote_copy(
            src_ref=ext_ref.at[2],
            dst_ref=ext_ref.at[2 - d],
            send_sem=send_b.at[i],
            recv_sem=recv_b.at[i],
            device_id=ring_places[i],
            device_id_type=MESH,
        )
        copy.start()
        copies.append(copy)
    for copy in copies:
        copy.wait()


def gather_blocks(velocity, ring):
    return pl.pallas_call(
        functools.partial(gather_kernel, ring),
        out_shape=jax.ShapeDtypeStruct((5, GROUP, 3, 8, 128), jnp.float32),
        in_specs=[VMEM_SPEC],
        out_specs=VMEM_SPEC,
        scratch_shapes=[
            pltpu.VMEM((GROUP, 3, 8, 128), jnp.float32),
            pltpu.SemaphoreType.DMA((GROUP - 1,)),
            pltpu.SemaphoreType.DMA((GROUP - 1,)),
            pltpu.SemaphoreType.DMA((4,)),
            pltpu.SemaphoreType.DMA((4,)),
        ],
        compiler_params=pltpu.CompilerParams(
            collective_id=0, has_side_effects=True, vmem_limit_bytes=16 * 2**20
        ),
        name="gather_blocks",
    )(velocity)


def wrap_rows(buf):
    buf[:, 0] = pltpu.roll(buf[:, 16].reshape(48, 128), 64, 1).reshape(3, 16, 128)
    buf[:, 17] = pltpu.roll(buf[:, 1].reshape(48, 128), 64, 1).reshape(3, 16, 128)


def section(src, base, dst, base_weight, weight):
    row = lax.broadcasted_iota(jnp.int32, (16, 128), 0)
    top, bottom = row == 15, row == 0
    even = weight * TIME_STEP * VISCOSITY
    odd = weight * TIME_STEP * 0.5
    own = weight * (1.0 - 6.0 * TIME_STEP * VISCOSITY)

    def one_row(r, carry):
        center = [src[c, r] for c in range(3)]
        ahead = [even - odd * center[j] for j in range(3)]
        behind = [2.0 * even - ahead[j] for j in range(3)]
        ahead[1] = jnp.where(top, 0.0, ahead[1])
        behind[1] = jnp.where(bottom, 0.0, behind[1])
        for c in range(3):
            value = own * center[c]
            x_part = ahead[0] * src[c, r + 1] + behind[0] * src[c, r - 1]
            y_part = ahead[1] * pltpu.roll(center[c], 15, 0) + behind[1] * pltpu.roll(center[c], 1, 0)
            z_part = ahead[2] * pltpu.roll(center[c], 127, 1) + behind[2] * pltpu.roll(center[c], 1, 1)
            if base is not None:
                value = value + base_weight * base[c, r]
            dst[c, r] = (value + x_part) + (y_part + z_part)
        return carry

    lax.fori_loop(1, 17, one_row, 0, unroll=4)
    wrap_rows(dst)


def solve_kernel(ext_ref, back_ref, coarse_ref, v, a, b):
    lane = lax.broadcasted_iota(jnp.int32, (24, 128), 1)
    for far in range(2):
        for y_half in range(2):
            for x in range(8):
                value = None
                for half in range(2):
                    for d in REACH:
                        piece = ext_ref[d + 2, 2 * (2 * half + far) + y_half].reshape(24, 128)
                        start = 64 * half + HALO + CHUNK * d
                        piece = pltpu.roll(piece, (start - CHUNK * x) % 128, 1)
                        if value is None:
                            value = piece
                        else:
                            first = max(start, 64 * half)
                            value = jnp.where(lane >= first, piece, value)
                v[:, 1 + 8 * far + x, 8 * y_half : 8 * y_half + 8, :] = value.reshape(3, 8, 128)
    wrap_rows(v)
    wide = lax.broadcasted_iota(jnp.int32, (16, 128), 1)

    def one_step(step, carry):
        section(v, None, a, 0.0, 1.0)
        section(a, v, b, 0.75, 0.25)
        section(b, v, v, ONE_THIRD, TWO_THIRDS)
        return carry

    coarse_ref[...] = jnp.zeros(coarse_ref.shape, jnp.float32)

    def one_snap(k, carry):
        lax.fori_loop(0, STEPS, one_step, 0)
        for c in range(3):
            for block in range(4):
                at = 1 + 4 * block
                total = (v[c, at] + v[c, at + 1]) + (v[c, at + 2] + v[c, at + 3])
                total = total + pltpu.roll(total, 127, 1)
                total = total + pltpu.roll(total, 126, 1)
                total = pltpu.roll(total * (1.0 / 16.0), k, 1)
                coarse_ref[c, block] = jnp.where(wide % 4 == k, total, coarse_ref[c, block])
        return carry

    lax.fori_loop(0, SNAPS, one_snap, 0)
    group = lax.broadcasted_iota(jnp.int32, (24, 128), 1) // CHUNK
    for half in range(2):
        for far in range(2):
            for y_half in range(2):
                value = None
                for x in range(8):
                    piece = v[:, 1 + 8 * far + x, 8 * y_half : 8 * y_half + 8, :].reshape(24, 128)
                    piece = pltpu.roll(piece, (CHUNK * x - 64 * half - HALO) % 128, 1)
                    value = piece if value is None else jnp.where(group >= x, piece, value)
                back_ref[2 * (2 * half + far) + y_half] = value.reshape(3, 8, 128)


def solve_window(ext):
    field = pltpu.VMEM((3, 18, 16, 128), jnp.float32)
    return pl.pallas_call(
        solve_kernel,
        out_shape=(
            jax.ShapeDtypeStruct((GROUP, 3, 8, 128), jnp.float32),
            jax.ShapeDtypeStruct((3, 4, 16, 128), jnp.float32),
        ),
        in_specs=[VMEM_SPEC],
        out_specs=(VMEM_SPEC, VMEM_SPEC),
        scratch_shapes=[field, field, field],
        compiler_params=pltpu.CompilerParams(vmem_limit_bytes=24 * 2**20),
        name="solve_window",
    )(ext)


def return_kernel(back_ref, coarse_ref, v_ref, pair_ref, landed, send_a, recv_a, send_b, recv_b):
    gx, gy, gz = lax.axis_index("gx"), lax.axis_index("gy"), lax.axis_index("gz")
    m = 2 * gx + gy
    mates = [((m + j) % GROUP) for j in range(1, GROUP)]
    mate_places = [(k // 2, k % 2, gz) for k in mates]
    meet(mate_places)
    partner = (gx, 1 - gy, gz)
    theirs = pl.multiple_of(8 * (1 - gy), 8)
    mine = pl.multiple_of(8 * gy, 8)
    coarse_copy = pltpu.make_async_remote_copy(
        src_ref=coarse_ref.at[:, :, pl.ds(theirs, 8), :],
        dst_ref=pair_ref.at[gy],
        send_sem=send_b,
        recv_sem=recv_b,
        device_id=partner,
        device_id_type=MESH,
    )
    coarse_copy.start()
    copies = []
    for j in range(1, GROUP):
        copy = pltpu.make_async_remote_copy(
            src_ref=back_ref.at[mates[j - 1]],
            dst_ref=landed.at[m],
            send_sem=send_a.at[j - 1],
            recv_sem=recv_a.at[j - 1],
            device_id=mate_places[j - 1],
            device_id_type=MESH,
        )
        copy.start()
        copies.append(copy)
    landed[m] = back_ref[m]
    pair_ref[gy] = coarse_ref[:, :, pl.ds(mine, 8), :]
    for copy in copies:
        copy.wait()
    rows = swap_groups([landed[k].reshape(24, 128) for k in range(GROUP)])
    for x in range(8):
        v_ref[:, x] = rows[x].reshape(3, 8, 128)
    coarse_copy.wait()


def return_blocks(back, coarse):
    return pl.pallas_call(
        return_kernel,
        out_shape=(
            jax.ShapeDtypeStruct((3, 8, 8, 128), jnp.float32),
            jax.ShapeDtypeStruct((2, 3, 4, 8, 128), jnp.float32),
        ),
        in_specs=[VMEM_SPEC, VMEM_SPEC],
        out_specs=(VMEM_SPEC, VMEM_SPEC),
        scratch_shapes=[
            pltpu.VMEM((GROUP, 3, 8, 128), jnp.float32),
            pltpu.SemaphoreType.DMA((GROUP - 1,)),
            pltpu.SemaphoreType.DMA((GROUP - 1,)),
            pltpu.SemaphoreType.DMA,
            pltpu.SemaphoreType.DMA,
        ],
        compiler_params=pltpu.CompilerParams(
            collective_id=1, has_side_effects=True, vmem_limit_bytes=16 * 2**20
        ),
        name="return_blocks",
    )(back, coarse)


def total_kernel(count_z, part_ref, out_ref, parts, sums, send_a, recv_a, send_b, recv_b, send_c, recv_c):
    gx, gy, gz = lax.axis_index("gx"), lax.axis_index("gy"), lax.axis_index("gz")
    m = 2 * gx + gy
    mates = [((m + j) % GROUP) for j in range(1, GROUP)]
    mate_places = [(k // 2, k % 2, gz) for k in mates]
    others = [((gz + j) % count_z) for j in range(1, count_z)]
    other_places = [(gx, gy, k) for k in others]
    meet(mate_places + other_places)

    def send(src, dst, send_sem, recv_sem, place):
        copy = pltpu.make_async_remote_copy(
            src_ref=src, dst_ref=dst, send_sem=send_sem, recv_sem=recv_sem,
            device_id=place, device_id_type=MESH,
        )
        copy.start()
        return copy

    copies = [
        send(part_ref.at[mates[j]], parts.at[m], send_a.at[j], recv_a.at[j], mate_places[j])
        for j in range(GROUP - 1)
    ]
    parts[m] = part_ref[m]
    for copy in copies:
        copy.wait()
    total = parts[0]
    for k in range(1, GROUP):
        total = total + parts[k]
    sums[gz] = total
    copies = [
        send(sums.at[gz], sums.at[gz], send_b.at[j], recv_b.at[j], other_places[j])
        for j in range(count_z - 1)
    ]
    for copy in copies:
        copy.wait()
    total = sums[0]
    for k in range(1, count_z):
        total = total + sums[k]
    out_ref[m] = total
    copies = [
        send(out_ref.at[m], out_ref.at[m], send_c.at[j], recv_c.at[j], mate_places[j])
        for j in range(GROUP - 1)
    ]
    for copy in copies:
        copy.wait()


def total_over_devices(part, count_z):
    rank = part.shape[0]
    rows = rank // GROUP
    sems = pltpu.SemaphoreType.DMA
    out = pl.pallas_call(
        functools.partial(total_kernel, count_z),
        out_shape=jax.ShapeDtypeStruct((GROUP, rows, rank), jnp.float32),
        in_specs=[VMEM_SPEC],
        out_specs=VMEM_SPEC,
        scratch_shapes=[
            pltpu.VMEM((GROUP, rows, rank), jnp.float32),
            pltpu.VMEM((count_z, rows, rank), jnp.float32),
            sems((GROUP - 1,)),
            sems((GROUP - 1,)),
            sems((count_z - 1,)),
            sems((count_z - 1,)),
            sems((GROUP - 1,)),
            sems((GROUP - 1,)),
        ],
        compiler_params=pltpu.CompilerParams(collective_id=2, has_side_effects=True),
        name="total_over_devices",
    )(part.reshape(GROUP, rows, rank))
    return out.reshape(rank, rank)


def omega_of(seed_matrix, snap_steps):
    picker = (
        snap_steps[:, None] == jnp.arange(seed_matrix.shape[0], dtype=jnp.int32)[None, :]
    ).astype(jnp.float32)
    return 0.5 * jnp.dot(picker, seed_matrix.astype(jnp.float32), precision=HIGHEST)


def finish(sketch_rows, gram_sum, rank_keep, shape):
    rank_total = shape[-1]
    lower_factor = jnp.linalg.cholesky(gram_sum)
    identity = jnp.eye(rank_total, dtype=jnp.float32)
    inverse = lax.linalg.triangular_solve(lower_factor, identity, left_side=True, lower=True).T
    total_rows = (
        sketch_rows.shape[0] * lax.axis_size("gx") * lax.axis_size("gy") * lax.axis_size("gz")
    )
    norm_scale = math.sqrt(total_rows)
    inside = (jnp.arange(rank_total, dtype=jnp.int32) < rank_keep[0]).astype(jnp.float32)
    mode_rows = norm_scale * jnp.dot(sketch_rows, inverse, precision=HIGHEST) * inside[None, :]
    factor = lower_factor.T * (1.0 / norm_scale) * inside[:, None] * inside[None, :]
    return mode_rows.reshape(shape), factor


def gram_of(sketch_rows):
    return lax.dot_general(
        sketch_rows, sketch_rows, (((0,), (0,)), ((), ())), precision=HIGHEST
    )


def by_chunks(velocity, sketch_prev, seed_matrix, snap_steps, rank_keep):
    rank_total = sketch_prev.shape[-1]
    count_z = lax.axis_size("gz")
    ext = gather_blocks(velocity, GROUP * count_z)
    back, coarse = solve_window(ext)
    current, pair = return_blocks(back, coarse)
    omega = omega_of(seed_matrix, snap_steps)
    spread = pair.reshape(2, 3, 4, 8, 2, 64)[..., HALO : HALO + CHUNK].reshape(2, 3, 4, 8, 2, 4, 4)
    snap_rows = jnp.transpose(spread, (6, 1, 3, 0, 5, 4, 2)).reshape(SNAPS, -1)
    sketch_rows = sketch_prev.reshape(-1, rank_total) + lax.dot_general(
        snap_rows, omega, (((0,), (0,)), ((), ())), precision=HIGHEST
    )
    gram_sum = total_over_devices(gram_of(sketch_rows), count_z)
    return (current,) + finish(sketch_rows, gram_sum, rank_keep, sketch_prev.shape)


def step_by_step(velocity, sketch_prev, seed_matrix, snap_steps, rank_keep):
    current = velocity
    collected = []
    for snap_index in range(SNAPS):
        for step_index in range(STEPS):
            current = step_by_section(current)
        local_snap = coarse_local(current)
        collected.append(lax.all_to_all(local_snap, "gx", split_axis=2, concat_axis=3, tiled=True))
    stacked = jnp.stack(collected)
    rank_total = sketch_prev.shape[-1]
    snap_rows = stacked.reshape(stacked.shape[0], -1)
    omega_rows = omega_of(seed_matrix, snap_steps)
    sketch_rows = sketch_prev.reshape(-1, rank_total) + lax.dot_general(
        snap_rows, omega_rows, (((0,), (0,)), ((), ())), precision=HIGHEST
    )
    gram_sum = lax.psum(gram_of(sketch_rows), ("gx", "gy", "gz"))
    return (current,) + finish(sketch_rows, gram_sum, rank_keep, sketch_prev.shape)


def on_device(velocity, sketch_prev, seed_matrix, snap_steps, rank_keep):
    fits = (
        (lax.axis_size("gx"), lax.axis_size("gy")) == (4, 2)
        and lax.axis_size("gz") >= 2
        and velocity.shape == (3, 8, 8, 128)
        and sketch_prev.shape == (3, 8, 1, 8, 8, 128)
    )
    run = by_chunks if fits else step_by_step
    return run(velocity, sketch_prev, seed_matrix, snap_steps, rank_keep)


def solution(mesh):
    placed = (P(None, "gx", "gy", "gz"), P(None, "gy", "gz", "gx", None, None), P(), P(), P())
    return jax.shard_map(
        on_device,
        mesh=mesh,
        in_specs=placed,
        out_specs=(P(None, "gx", "gy", "gz"), P(None, "gy", "gz", "gx", None, None), P()),
        check_vma=False,
    )
```

```python
import functools
import math

import jax
import jax.numpy as jnp
from jax import lax
from jax.experimental import pallas as pl
from jax.experimental.pallas import tpu as pltpu
from jax.sharding import PartitionSpec as P

MESH = pl.DeviceIdType.MESH
VMEM_SPEC = pl.BlockSpec(memory_space=pltpu.VMEM)

SNAPS = 4
STEPS = 2


TIME_STEP = 0.1
VISCOSITY = 0.4
ONE_THIRD = 1.0 / 3.0
TWO_THIRDS = 2.0 / 3.0
HIGHEST = lax.Precision.HIGHEST


def extended(block, sides, width):
    for axis, dim in sides:
        count = lax.axis_size(axis)
        forward = [(i, i + 1) for i in range(count - 1)]
        forward.append((count - 1, 0))
        backward = [(target, source) for source, target in forward]
        low = lax.ppermute(
            lax.slice_in_dim(block, block.shape[dim] - width, None, axis=dim), axis, forward
        )
        high = lax.ppermute(lax.slice_in_dim(block, 0, width, axis=dim), axis, backward)
        block = jnp.concatenate([low, block, high], axis=dim)
    return block


def tendency(padded):
    center = padded[:, 1:-1, 1:-1, 1:-1]
    forward = (padded[:, 2:, 1:-1, 1:-1], padded[:, 1:-1, 2:, 1:-1], padded[:, 1:-1, 1:-1, 2:])
    backward = (padded[:, :-2, 1:-1, 1:-1], padded[:, 1:-1, :-2, 1:-1], padded[:, 1:-1, 1:-1, :-2])
    convect = (
        center[0:1] * (forward[0] - backward[0])
        + center[1:2] * (forward[1] - backward[1])
        + center[2:3] * (forward[2] - backward[2])
    )
    spread = (
        forward[0]
        + backward[0]
        + forward[1]
        + backward[1]
        + forward[2]
        + backward[2]
        - 6.0 * center
    )
    return -0.5 * convect + VISCOSITY * spread


def with_walls(padded, margin):
    cells_y = padded.shape[2] - 2 * margin
    wall_rows = (
        lax.axis_index("gy") * cells_y - margin + jnp.arange(cells_y + 2 * margin, dtype=jnp.int32)
    )
    inside = ((wall_rows >= 0) & (wall_rows < lax.axis_size("gy") * cells_y)).astype(jnp.float32)
    return padded * inside[None, None, :, None]


def faces_padded(current):
    return with_walls(extended(current, (("gx", 1), ("gy", 2), ("gz", 3)), 1), 1)


def step_by_section(current):
    first_section = current + TIME_STEP * tendency(faces_padded(current))
    second_section = 0.75 * current + 0.25 * (
        first_section + TIME_STEP * tendency(faces_padded(first_section))
    )
    return ONE_THIRD * current + TWO_THIRDS * (
        second_section + TIME_STEP * tendency(faces_padded(second_section))
    )


def coarse_local(current):
    cells_x = current.shape[1]
    cells_y = current.shape[2]
    cells_z = current.shape[3]
    blocks = current.reshape(3, cells_x // 4, 4, cells_y, cells_z // 4, 4)
    return jnp.transpose(jnp.mean(blocks, axis=(2, 5)), (0, 2, 3, 1))


GROUP = 8
CHUNK = 16
HALO = 24
REACH = (-2, -1, 0, 1, 2)


def place_of(n):
    m = n % GROUP
    return (m // 2, m % 2, n // GROUP)


def swap_groups(rows):
    rows = list(rows)
    lane = lax.broadcasted_iota(jnp.int32, rows[0].shape, 1)
    for step in (1, 2, 4):
        low = (lane // (CHUNK * step)) % 2 == 0
        for i in range(GROUP):
            if i & step:
                continue
            first, second = rows[i], rows[i | step]
            rows[i] = jnp.where(low, first, pltpu.roll(second, CHUNK * step, 1))
            rows[i | step] = jnp.where(low, pltpu.roll(first, 128 - CHUNK * step, 1), second)
    return rows


def meet(places):
    barrier = pltpu.get_barrier_semaphore()
    for place in places:
        pl.semaphore_signal(barrier, inc=1, device_id=place, device_id_type=MESH)
    pl.semaphore_wait(barrier, len(places))


def gather_kernel(ring, v_ref, ext_ref, packed, send_a, recv_a, send_b, recv_b):
    gx, gy, gz = lax.axis_index("gx"), lax.axis_index("gy"), lax.axis_index("gz")
    m = 2 * gx + gy
    n = GROUP * gz + m
    mates = [((m + j) % GROUP) for j in range(1, GROUP)]
    mate_places = [(k // 2, k % 2, gz) for k in mates]
    offsets = [d for d in REACH if d != 0]
    ring_places = [place_of((n + d + ring) % ring) for d in offsets]
    rows = swap_groups([v_ref[:, x].reshape(24, 128) for x in range(8)])
    for k in range(GROUP):
        packed[k] = rows[k].reshape(3, 8, 128)
    meet(mate_places + ring_places)
    copies = []
    for j in range(1, GROUP):
        copy = pltpu.make_async_remote_copy(
            src_ref=packed.at[mates[j - 1]],
            dst_ref=ext_ref.at[2, m],
            send_sem=send_a.at[j - 1],
            recv_sem=recv_a.at[j - 1],
            device_id=mate_places[j - 1],
            device_id_type=MESH,
        )
        copy.start()
        copies.append(copy)
    ext_ref[2, m] = packed[m]
    for copy in copies:
        copy.wait()
    copies = []
    for i, d in enumerate(offsets):
        copy = pltpu.make_async_remote_copy(
            src_ref=ext_ref.at[2],
            dst_ref=ext_ref.at[2 - d],
            send_sem=send_b.at[i],
            recv_sem=recv_b.at[i],
            device_id=ring_places[i],
            device_id_type=MESH,
        )
        copy.start()
        copies.append(copy)
    for copy in copies:
        copy.wait()


def gather_blocks(velocity, ring):
    return pl.pallas_call(
        functools.partial(gather_kernel, ring),
        out_shape=jax.ShapeDtypeStruct((5, GROUP, 3, 8, 128), jnp.float32),
        in_specs=[VMEM_SPEC],
        out_specs=VMEM_SPEC,
        scratch_shapes=[
            pltpu.VMEM((GROUP, 3, 8, 128), jnp.float32),
            pltpu.SemaphoreType.DMA((GROUP - 1,)),
            pltpu.SemaphoreType.DMA((GROUP - 1,)),
            pltpu.SemaphoreType.DMA((4,)),
            pltpu.SemaphoreType.DMA((4,)),
        ],
        compiler_params=pltpu.CompilerParams(
            collective_id=0, has_side_effects=True, vmem_limit_bytes=16 * 2**20
        ),
        name="gather_blocks",
    )(velocity)


def wrap_rows(buf):
    buf[:, 0] = pltpu.roll(buf[:, 16].reshape(48, 128), 64, 1).reshape(3, 16, 128)
    buf[:, 17] = pltpu.roll(buf[:, 1].reshape(48, 128), 64, 1).reshape(3, 16, 128)


def section(src, base, dst, base_weight, weight):
    row = lax.broadcasted_iota(jnp.int32, (16, 128), 0)
    top, bottom = row == 15, row == 0
    even = weight * TIME_STEP * VISCOSITY
    odd = weight * TIME_STEP * 0.5
    own = weight * (1.0 - 6.0 * TIME_STEP * VISCOSITY)

    def one_row(r, carry):
        center = [src[c, r] for c in range(3)]
        ahead = [even - odd * center[j] for j in range(3)]
        behind = [2.0 * even - ahead[j] for j in range(3)]
        ahead[1] = jnp.where(top, 0.0, ahead[1])
        behind[1] = jnp.where(bottom, 0.0, behind[1])
        for c in range(3):
            value = own * center[c]
            x_part = ahead[0] * src[c, r + 1] + behind[0] * src[c, r - 1]
            y_part = ahead[1] * pltpu.roll(center[c], 15, 0) + behind[1] * pltpu.roll(center[c], 1, 0)
            z_part = ahead[2] * pltpu.roll(center[c], 127, 1) + behind[2] * pltpu.roll(center[c], 1, 1)
            if base is not None:
                value = value + base_weight * base[c, r]
            dst[c, r] = (value + x_part) + (y_part + z_part)
        return carry

    lax.fori_loop(1, 17, one_row, 0, unroll=4)
    wrap_rows(dst)


def solve_kernel(ext_ref, back_ref, coarse_ref, v, a, b):
    lane = lax.broadcasted_iota(jnp.int32, (24, 128), 1)
    for far in range(2):
        for y_half in range(2):
            for x in range(8):
                value = None
                for half in range(2):
                    for d in REACH:
                        piece = ext_ref[d + 2, 2 * (2 * half + far) + y_half].reshape(24, 128)
                        start = 64 * half + HALO + CHUNK * d
                        piece = pltpu.roll(piece, (start - CHUNK * x) % 128, 1)
                        if value is None:
                            value = piece
                        else:
                            first = max(start, 64 * half)
                            value = jnp.where(lane >= first, piece, value)
                v[:, 1 + 8 * far + x, 8 * y_half : 8 * y_half + 8, :] = value.reshape(3, 8, 128)
    wrap_rows(v)
    wide = lax.broadcasted_iota(jnp.int32, (16, 128), 1)

    def one_step(step, carry):
        section(v, None, a, 0.0, 1.0)
        section(a, v, b, 0.75, 0.25)
        section(b, v, v, ONE_THIRD, TWO_THIRDS)
        return carry

    coarse_ref[...] = jnp.zeros(coarse_ref.shape, jnp.float32)

    def one_snap(k, carry):
        lax.fori_loop(0, STEPS, one_step, 0)
        for c in range(3):
            for block in range(4):
                at = 1 + 4 * block
                total = (v[c, at] + v[c, at + 1]) + (v[c, at + 2] + v[c, at + 3])
                total = total + pltpu.roll(total, 127, 1)
                total = total + pltpu.roll(total, 126, 1)
                total = pltpu.roll(total * (1.0 / 16.0), k, 1)
                coarse_ref[c, block] = jnp.where(wide % 4 == k, total, coarse_ref[c, block])
        return carry

    lax.fori_loop(0, SNAPS, one_snap, 0)
    group = lax.broadcasted_iota(jnp.int32, (24, 128), 1) // CHUNK
    for half in range(2):
        for far in range(2):
            for y_half in range(2):
                value = None
                for x in range(8):
                    piece = v[:, 1 + 8 * far + x, 8 * y_half : 8 * y_half + 8, :].reshape(24, 128)
                    piece = pltpu.roll(piece, (CHUNK * x - 64 * half - HALO) % 128, 1)
                    value = piece if value is None else jnp.where(group >= x, piece, value)
                back_ref[2 * (2 * half + far) + y_half] = value.reshape(3, 8, 128)


def solve_window(ext):
    field = pltpu.VMEM((3, 18, 16, 128), jnp.float32)
    return pl.pallas_call(
        solve_kernel,
        out_shape=(
            jax.ShapeDtypeStruct((GROUP, 3, 8, 128), jnp.float32),
            jax.ShapeDtypeStruct((3, 4, 16, 128), jnp.float32),
        ),
        in_specs=[VMEM_SPEC],
        out_specs=(VMEM_SPEC, VMEM_SPEC),
        scratch_shapes=[field, field, field],
        compiler_params=pltpu.CompilerParams(vmem_limit_bytes=24 * 2**20),
        name="solve_window",
    )(ext)


def return_kernel(back_ref, coarse_ref, v_ref, pair_ref, landed, send_a, recv_a, send_b, recv_b):
    gx, gy, gz = lax.axis_index("gx"), lax.axis_index("gy"), lax.axis_index("gz")
    m = 2 * gx + gy
    mates = [((m + j) % GROUP) for j in range(1, GROUP)]
    mate_places = [(k // 2, k % 2, gz) for k in mates]
    meet(mate_places)
    partner = (gx, 1 - gy, gz)
    theirs = pl.multiple_of(8 * (1 - gy), 8)
    mine = pl.multiple_of(8 * gy, 8)
    coarse_copy = pltpu.make_async_remote_copy(
        src_ref=coarse_ref.at[:, :, pl.ds(theirs, 8), :],
        dst_ref=pair_ref.at[gy],
        send_sem=send_b,
        recv_sem=recv_b,
        device_id=partner,
        device_id_type=MESH,
    )
    coarse_copy.start()
    copies = []
    for j in range(1, GROUP):
        copy = pltpu.make_async_remote_copy(
            src_ref=back_ref.at[mates[j - 1]],
            dst_ref=landed.at[m],
            send_sem=send_a.at[j - 1],
            recv_sem=recv_a.at[j - 1],
            device_id=mate_places[j - 1],
            device_id_type=MESH,
        )
        copy.start()
        copies.append(copy)
    landed[m] = back_ref[m]
    pair_ref[gy] = coarse_ref[:, :, pl.ds(mine, 8), :]
    for copy in copies:
        copy.wait()
    rows = swap_groups([landed[k].reshape(24, 128) for k in range(GROUP)])
    for x in range(8):
        v_ref[:, x] = rows[x].reshape(3, 8, 128)
    coarse_copy.wait()


def return_blocks(back, coarse):
    return pl.pallas_call(
        return_kernel,
        out_shape=(
            jax.ShapeDtypeStruct((3, 8, 8, 128), jnp.float32),
            jax.ShapeDtypeStruct((2, 3, 4, 8, 128), jnp.float32),
        ),
        in_specs=[VMEM_SPEC, VMEM_SPEC],
        out_specs=(VMEM_SPEC, VMEM_SPEC),
        scratch_shapes=[
            pltpu.VMEM((GROUP, 3, 8, 128), jnp.float32),
            pltpu.SemaphoreType.DMA((GROUP - 1,)),
            pltpu.SemaphoreType.DMA((GROUP - 1,)),
            pltpu.SemaphoreType.DMA,
            pltpu.SemaphoreType.DMA,
        ],
        compiler_params=pltpu.CompilerParams(
            collective_id=1, has_side_effects=True, vmem_limit_bytes=16 * 2**20
        ),
        name="return_blocks",
    )(back, coarse)


def total_kernel(count_z, part_ref, out_ref, parts, sums, send_a, recv_a, send_b, recv_b, send_c, recv_c):
    gx, gy, gz = lax.axis_index("gx"), lax.axis_index("gy"), lax.axis_index("gz")
    m = 2 * gx + gy
    mates = [((m + j) % GROUP) for j in range(1, GROUP)]
    mate_places = [(k // 2, k % 2, gz) for k in mates]
    others = [((gz + j) % count_z) for j in range(1, count_z)]
    other_places = [(gx, gy, k) for k in others]
    meet(mate_places + other_places)

    def send(src, dst, send_sem, recv_sem, place):
        copy = pltpu.make_async_remote_copy(
            src_ref=src, dst_ref=dst, send_sem=send_sem, recv_sem=recv_sem,
            device_id=place, device_id_type=MESH,
        )
        copy.start()
        return copy

    copies = [
        send(part_ref.at[mates[j]], parts.at[m], send_a.at[j], recv_a.at[j], mate_places[j])
        for j in range(GROUP - 1)
    ]
    parts[m] = part_ref[m]
    for copy in copies:
        copy.wait()
    total = parts[0]
    for k in range(1, GROUP):
        total = total + parts[k]
    sums[gz] = total
    copies = [
        send(sums.at[gz], sums.at[gz], send_b.at[j], recv_b.at[j], other_places[j])
        for j in range(count_z - 1)
    ]
    for copy in copies:
        copy.wait()
    total = sums[0]
    for k in range(1, count_z):
        total = total + sums[k]
    out_ref[m] = total
    copies = [
        send(out_ref.at[m], out_ref.at[m], send_c.at[j], recv_c.at[j], mate_places[j])
        for j in range(GROUP - 1)
    ]
    for copy in copies:
        copy.wait()


def total_over_devices(part, count_z):
    rank = part.shape[0]
    rows = rank // GROUP
    sems = pltpu.SemaphoreType.DMA
    out = pl.pallas_call(
        functools.partial(total_kernel, count_z),
        out_shape=jax.ShapeDtypeStruct((GROUP, rows, rank), jnp.float32),
        in_specs=[VMEM_SPEC],
        out_specs=VMEM_SPEC,
        scratch_shapes=[
            pltpu.VMEM((GROUP, rows, rank), jnp.float32),
            pltpu.VMEM((count_z, rows, rank), jnp.float32),
            sems((GROUP - 1,)),
            sems((GROUP - 1,)),
            sems((count_z - 1,)),
            sems((count_z - 1,)),
            sems((GROUP - 1,)),
            sems((GROUP - 1,)),
        ],
        compiler_params=pltpu.CompilerParams(collective_id=2, has_side_effects=True),
        name="total_over_devices",
    )(part.reshape(GROUP, rows, rank))
    return out.reshape(rank, rank)


def omega_of(seed_matrix, snap_steps):
    picker = (
        snap_steps[:, None] == jnp.arange(seed_matrix.shape[0], dtype=jnp.int32)[None, :]
    ).astype(jnp.float32)
    return 0.5 * jnp.dot(picker, seed_matrix.astype(jnp.float32), precision=HIGHEST)


def factor_kernel(norm_scale, keep_ref, gram_ref, sketch_ref, rows_ref, factor_ref, unit):
    rank = gram_ref.shape[0]
    tiles = rank // 8
    down = lax.broadcasted_iota(jnp.int32, (8, rank), 0)
    lane = lax.broadcasted_iota(jnp.int32, (8, rank), 1)
    left = [gram_ref[8 * t : 8 * t + 8, :] for t in range(tiles)]
    right = [(lane == down + 8 * t).astype(jnp.float32) for t in range(tiles)]

    def spread(tile, i):
        return jnp.broadcast_to(tile[i : i + 1, :], (8, rank))

    for k in range(0, rank, 2):
        home, i = k // 8, k % 8
        first = [jnp.broadcast_to(left[t][:, k : k + 1], (8, rank)) for t in range(home, tiles)]
        second = [jnp.broadcast_to(left[t][:, k + 1 : k + 2], (8, rank)) for t in range(home, tiles)]
        p, q, s = spread(first[0], i), spread(second[0], i), spread(second[0], i + 1)
        inv_p = 1.0 / p
        ratio = q * inv_p
        inv_s = 1.0 / (s - ratio * q)
        row_a, row_za = spread(left[home], i), spread(right[home], i)
        row_b = spread(left[home], i + 1) - ratio * row_a
        row_zb = spread(right[home], i + 1) - ratio * row_za
        for t in range(home, tiles):
            m_a = first[t - home] * inv_p
            m_b = (second[t - home] - first[t - home] * ratio) * inv_s
            if t == home:
                m_a = jnp.where(down > i, m_a, 0.0)
                m_b = jnp.where(down > i + 1, m_b, 0.0)
            left[t] = left[t] - m_a * row_a - m_b * row_b
            right[t] = right[t] - m_a * row_za - m_b * row_zb
    keep = keep_ref[0]
    for t in range(tiles):
        at = down + 8 * t
        pivot = jnp.sum(jnp.where(lane == at, left[t], 0.0), axis=1, keepdims=True)
        scale = lax.rsqrt(pivot)
        inside = at < keep
        factor_ref[8 * t : 8 * t + 8, :] = jnp.where(
            inside & (lane < keep) & (lane >= at), left[t] * (scale * (1.0 / norm_scale)), 0.0
        )
        unit[8 * t : 8 * t + 8, :] = jnp.where(inside, right[t] * (scale * norm_scale), 0.0)
    rows_ref[...] = lax.dot_general(
        sketch_ref[...], unit[...], (((1,), (1,)), ((), ())),
        precision=HIGHEST, preferred_element_type=jnp.float32,
    )


def finish(sketch_rows, gram_sum, rank_keep, shape):
    rank = shape[-1]
    total_rows = (
        sketch_rows.shape[0] * lax.axis_size("gx") * lax.axis_size("gy") * lax.axis_size("gz")
    )
    mode_rows, factor = pl.pallas_call(
        functools.partial(factor_kernel, math.sqrt(total_rows)),
        out_shape=(
            jax.ShapeDtypeStruct(sketch_rows.shape, jnp.float32),
            jax.ShapeDtypeStruct((rank, rank), jnp.float32),
        ),
        in_specs=[pl.BlockSpec(memory_space=pltpu.SMEM), VMEM_SPEC, VMEM_SPEC],
        out_specs=(VMEM_SPEC, VMEM_SPEC),
        scratch_shapes=[pltpu.VMEM((rank, rank), jnp.float32)],
        compiler_params=pltpu.CompilerParams(vmem_limit_bytes=24 * 2**20),
        name="factor_and_rows",
    )(rank_keep, gram_sum, sketch_rows)
    return mode_rows.reshape(shape), factor


def gram_of(sketch_rows):
    return lax.dot_general(
        sketch_rows, sketch_rows, (((0,), (0,)), ((), ())), precision=HIGHEST
    )


def by_chunks(velocity, sketch_prev, seed_matrix, snap_steps, rank_keep):
    rank_total = sketch_prev.shape[-1]
    count_z = lax.axis_size("gz")
    ext = gather_blocks(velocity, GROUP * count_z)
    back, coarse = solve_window(ext)
    current, pair = return_blocks(back, coarse)
    omega = omega_of(seed_matrix, snap_steps)
    spread = pair.reshape(2, 3, 4, 8, 2, 64)[..., HALO : HALO + CHUNK].reshape(2, 3, 4, 8, 2, 4, 4)
    snap_rows = jnp.transpose(spread, (6, 1, 3, 0, 5, 4, 2)).reshape(SNAPS, -1)
    sketch_rows = sketch_prev.reshape(-1, rank_total) + lax.dot_general(
        snap_rows, omega, (((0,), (0,)), ((), ())), precision=HIGHEST
    )
    gram_sum = total_over_devices(gram_of(sketch_rows), count_z)
    return (current,) + finish(sketch_rows, gram_sum, rank_keep, sketch_prev.shape)


def step_by_step(velocity, sketch_prev, seed_matrix, snap_steps, rank_keep):
    current = velocity
    collected = []
    for snap_index in range(SNAPS):
        for step_index in range(STEPS):
            current = step_by_section(current)
        local_snap = coarse_local(current)
        collected.append(lax.all_to_all(local_snap, "gx", split_axis=2, concat_axis=3, tiled=True))
    stacked = jnp.stack(collected)
    rank_total = sketch_prev.shape[-1]
    snap_rows = stacked.reshape(stacked.shape[0], -1)
    omega_rows = omega_of(seed_matrix, snap_steps)
    sketch_rows = sketch_prev.reshape(-1, rank_total) + lax.dot_general(
        snap_rows, omega_rows, (((0,), (0,)), ((), ())), precision=HIGHEST
    )
    gram_sum = lax.psum(gram_of(sketch_rows), ("gx", "gy", "gz"))
    return (current,) + finish(sketch_rows, gram_sum, rank_keep, sketch_prev.shape)


def on_device(velocity, sketch_prev, seed_matrix, snap_steps, rank_keep):
    fits = (
        (lax.axis_size("gx"), lax.axis_size("gy")) == (4, 2)
        and lax.axis_size("gz") >= 2
        and velocity.shape == (3, 8, 8, 128)
        and sketch_prev.shape == (3, 8, 1, 8, 8, 128)
    )
    run = by_chunks if fits else step_by_step
    return run(velocity, sketch_prev, seed_matrix, snap_steps, rank_keep)


def solution(mesh):
    placed = (P(None, "gx", "gy", "gz"), P(None, "gy", "gz", "gx", None, None), P(), P(), P())
    return jax.shard_map(
        on_device,
        mesh=mesh,
        in_specs=placed,
        out_specs=(P(None, "gx", "gy", "gz"), P(None, "gy", "gz", "gx", None, None), P()),
        check_vma=False,
    )
```

```python
import functools
import math

import jax
import jax.numpy as jnp
from jax import lax
from jax.experimental import pallas as pl
from jax.experimental.pallas import tpu as pltpu
from jax.sharding import PartitionSpec as P

MESH = pl.DeviceIdType.MESH
VMEM_SPEC = pl.BlockSpec(memory_space=pltpu.VMEM)

SNAPS = 4
STEPS = 2


TIME_STEP = 0.1
VISCOSITY = 0.4
ONE_THIRD = 1.0 / 3.0
TWO_THIRDS = 2.0 / 3.0
HIGHEST = lax.Precision.HIGHEST


def extended(block, sides, width):
    for axis, dim in sides:
        count = lax.axis_size(axis)
        forward = [(i, i + 1) for i in range(count - 1)]
        forward.append((count - 1, 0))
        backward = [(target, source) for source, target in forward]
        low = lax.ppermute(
            lax.slice_in_dim(block, block.shape[dim] - width, None, axis=dim), axis, forward
        )
        high = lax.ppermute(lax.slice_in_dim(block, 0, width, axis=dim), axis, backward)
        block = jnp.concatenate([low, block, high], axis=dim)
    return block


def tendency(padded):
    center = padded[:, 1:-1, 1:-1, 1:-1]
    forward = (padded[:, 2:, 1:-1, 1:-1], padded[:, 1:-1, 2:, 1:-1], padded[:, 1:-1, 1:-1, 2:])
    backward = (padded[:, :-2, 1:-1, 1:-1], padded[:, 1:-1, :-2, 1:-1], padded[:, 1:-1, 1:-1, :-2])
    convect = (
        center[0:1] * (forward[0] - backward[0])
        + center[1:2] * (forward[1] - backward[1])
        + center[2:3] * (forward[2] - backward[2])
    )
    spread = (
        forward[0]
        + backward[0]
        + forward[1]
        + backward[1]
        + forward[2]
        + backward[2]
        - 6.0 * center
    )
    return -0.5 * convect + VISCOSITY * spread


def with_walls(padded, margin):
    cells_y = padded.shape[2] - 2 * margin
    wall_rows = (
        lax.axis_index("gy") * cells_y - margin + jnp.arange(cells_y + 2 * margin, dtype=jnp.int32)
    )
    inside = ((wall_rows >= 0) & (wall_rows < lax.axis_size("gy") * cells_y)).astype(jnp.float32)
    return padded * inside[None, None, :, None]


def faces_padded(current):
    return with_walls(extended(current, (("gx", 1), ("gy", 2), ("gz", 3)), 1), 1)


def step_by_section(current):
    first_section = current + TIME_STEP * tendency(faces_padded(current))
    second_section = 0.75 * current + 0.25 * (
        first_section + TIME_STEP * tendency(faces_padded(first_section))
    )
    return ONE_THIRD * current + TWO_THIRDS * (
        second_section + TIME_STEP * tendency(faces_padded(second_section))
    )


def coarse_local(current):
    cells_x = current.shape[1]
    cells_y = current.shape[2]
    cells_z = current.shape[3]
    blocks = current.reshape(3, cells_x // 4, 4, cells_y, cells_z // 4, 4)
    return jnp.transpose(jnp.mean(blocks, axis=(2, 5)), (0, 2, 3, 1))


GROUP = 8
CHUNK = 16
HALO = 24
REACH = (-2, -1, 0, 1, 2)


def place_of(n):
    m = n % GROUP
    return (m // 2, m % 2, n // GROUP)


def swap_groups(rows):
    rows = list(rows)
    lane = lax.broadcasted_iota(jnp.int32, rows[0].shape, 1)
    for step in (1, 2, 4):
        low = (lane // (CHUNK * step)) % 2 == 0
        for i in range(GROUP):
            if i & step:
                continue
            first, second = rows[i], rows[i | step]
            rows[i] = jnp.where(low, first, pltpu.roll(second, CHUNK * step, 1))
            rows[i | step] = jnp.where(low, pltpu.roll(first, 128 - CHUNK * step, 1), second)
    return rows


def greet(places):
    barrier = pltpu.get_barrier_semaphore()
    for place in places:
        pl.semaphore_signal(barrier, inc=1, device_id=place, device_id_type=MESH)


def meet(places):
    pl.semaphore_wait(pltpu.get_barrier_semaphore(), len(places))


def gather_kernel(ring, v_ref, ext_ref, packed, send_a, recv_a, send_b, recv_b):
    gx, gy, gz = lax.axis_index("gx"), lax.axis_index("gy"), lax.axis_index("gz")
    m = 2 * gx + gy
    n = GROUP * gz + m
    mates = [((m + j) % GROUP) for j in range(1, GROUP)]
    mate_places = [(k // 2, k % 2, gz) for k in mates]
    offsets = [d for d in REACH if d != 0]
    ring_places = [place_of((n + d + ring) % ring) for d in offsets]
    greet(mate_places + ring_places)
    rows = swap_groups([v_ref[:, x].reshape(24, 128) for x in range(8)])
    for k in range(GROUP):
        packed[k] = rows[k].reshape(3, 8, 128)
    meet(mate_places + ring_places)
    copies = []
    for j in range(1, GROUP):
        copy = pltpu.make_async_remote_copy(
            src_ref=packed.at[mates[j - 1]],
            dst_ref=ext_ref.at[2, m],
            send_sem=send_a.at[j - 1],
            recv_sem=recv_a.at[j - 1],
            device_id=mate_places[j - 1],
            device_id_type=MESH,
        )
        copy.start()
        copies.append(copy)
    ext_ref[2, m] = packed[m]
    for copy in copies:
        copy.wait()
    copies = []
    for i, d in enumerate(offsets):
        copy = pltpu.make_async_remote_copy(
            src_ref=ext_ref.at[2],
            dst_ref=ext_ref.at[2 - d],
            send_sem=send_b.at[i],
            recv_sem=recv_b.at[i],
            device_id=ring_places[i],
            device_id_type=MESH,
        )
        copy.start()
        copies.append(copy)
    for copy in copies:
        copy.wait()


def gather_blocks(velocity, ring):
    return pl.pallas_call(
        functools.partial(gather_kernel, ring),
        out_shape=jax.ShapeDtypeStruct((5, GROUP, 3, 8, 128), jnp.float32),
        in_specs=[VMEM_SPEC],
        out_specs=VMEM_SPEC,
        scratch_shapes=[
            pltpu.VMEM((GROUP, 3, 8, 128), jnp.float32),
            pltpu.SemaphoreType.DMA((GROUP - 1,)),
            pltpu.SemaphoreType.DMA((GROUP - 1,)),
            pltpu.SemaphoreType.DMA((4,)),
            pltpu.SemaphoreType.DMA((4,)),
        ],
        compiler_params=pltpu.CompilerParams(
            collective_id=0, has_side_effects=True, vmem_limit_bytes=16 * 2**20
        ),
        name="gather_blocks",
    )(velocity)


def wrap_rows(buf):
    buf[:, 0] = pltpu.roll(buf[:, 16].reshape(48, 128), 64, 1).reshape(3, 16, 128)
    buf[:, 17] = pltpu.roll(buf[:, 1].reshape(48, 128), 64, 1).reshape(3, 16, 128)


def section(src, base, dst, base_weight, weight):
    row = lax.broadcasted_iota(jnp.int32, (16, 128), 0)
    top, bottom = row == 15, row == 0
    even = weight * TIME_STEP * VISCOSITY
    odd = weight * TIME_STEP * 0.5
    own = weight * (1.0 - 6.0 * TIME_STEP * VISCOSITY)

    def one_row(r, carry):
        center = [src[c, r] for c in range(3)]
        ahead = [even - odd * center[j] for j in range(3)]
        behind = [2.0 * even - ahead[j] for j in range(3)]
        ahead[1] = jnp.where(top, 0.0, ahead[1])
        behind[1] = jnp.where(bottom, 0.0, behind[1])
        for c in range(3):
            value = own * center[c]
            x_part = ahead[0] * src[c, r + 1] + behind[0] * src[c, r - 1]
            y_part = ahead[1] * pltpu.roll(center[c], 15, 0) + behind[1] * pltpu.roll(center[c], 1, 0)
            z_part = ahead[2] * pltpu.roll(center[c], 127, 1) + behind[2] * pltpu.roll(center[c], 1, 1)
            if base is not None:
                value = value + base_weight * base[c, r]
            dst[c, r] = (value + x_part) + (y_part + z_part)
        return carry

    lax.fori_loop(1, 17, one_row, 0, unroll=4)
    wrap_rows(dst)


def solve_kernel(ext_ref, back_ref, coarse_ref, v, a, b):
    lane = lax.broadcasted_iota(jnp.int32, (24, 128), 1)
    for far in range(2):
        for y_half in range(2):
            for x in range(8):
                value = None
                for half in range(2):
                    for d in REACH:
                        piece = ext_ref[d + 2, 2 * (2 * half + far) + y_half].reshape(24, 128)
                        start = 64 * half + HALO + CHUNK * d
                        piece = pltpu.roll(piece, (start - CHUNK * x) % 128, 1)
                        if value is None:
                            value = piece
                        else:
                            first = max(start, 64 * half)
                            value = jnp.where(lane >= first, piece, value)
                v[:, 1 + 8 * far + x, 8 * y_half : 8 * y_half + 8, :] = value.reshape(3, 8, 128)
    wrap_rows(v)
    wide = lax.broadcasted_iota(jnp.int32, (16, 128), 1)

    def one_step(step, carry):
        section(v, None, a, 0.0, 1.0)
        section(a, v, b, 0.75, 0.25)
        section(b, v, v, ONE_THIRD, TWO_THIRDS)
        return carry

    coarse_ref[...] = jnp.zeros(coarse_ref.shape, jnp.float32)

    def one_snap(k, carry):
        lax.fori_loop(0, STEPS, one_step, 0)
        for c in range(3):
            for block in range(4):
                at = 1 + 4 * block
                total = (v[c, at] + v[c, at + 1]) + (v[c, at + 2] + v[c, at + 3])
                total = total + pltpu.roll(total, 127, 1)
                total = total + pltpu.roll(total, 126, 1)
                total = pltpu.roll(total * (1.0 / 16.0), k, 1)
                coarse_ref[c, block] = jnp.where(wide % 4 == k, total, coarse_ref[c, block])
        return carry

    lax.fori_loop(0, SNAPS, one_snap, 0)
    group = lax.broadcasted_iota(jnp.int32, (24, 128), 1) // CHUNK
    for half in range(2):
        for far in range(2):
            for y_half in range(2):
                value = None
                for x in range(8):
                    piece = v[:, 1 + 8 * far + x, 8 * y_half : 8 * y_half + 8, :].reshape(24, 128)
                    piece = pltpu.roll(piece, (CHUNK * x - 64 * half - HALO) % 128, 1)
                    value = piece if value is None else jnp.where(group >= x, piece, value)
                back_ref[2 * (2 * half + far) + y_half] = value.reshape(3, 8, 128)


def solve_window(ext):
    field = pltpu.VMEM((3, 18, 16, 128), jnp.float32)
    return pl.pallas_call(
        solve_kernel,
        out_shape=(
            jax.ShapeDtypeStruct((GROUP, 3, 8, 128), jnp.float32),
            jax.ShapeDtypeStruct((3, 4, 16, 128), jnp.float32),
        ),
        in_specs=[VMEM_SPEC],
        out_specs=(VMEM_SPEC, VMEM_SPEC),
        scratch_shapes=[field, field, field],
        compiler_params=pltpu.CompilerParams(vmem_limit_bytes=24 * 2**20),
        name="solve_window",
    )(ext)


def return_kernel(back_ref, coarse_ref, v_ref, pair_ref, landed, send_a, recv_a, send_b, recv_b):
    gx, gy, gz = lax.axis_index("gx"), lax.axis_index("gy"), lax.axis_index("gz")
    m = 2 * gx + gy
    mates = [((m + j) % GROUP) for j in range(1, GROUP)]
    mate_places = [(k // 2, k % 2, gz) for k in mates]
    greet(mate_places)
    meet(mate_places)
    partner = (gx, 1 - gy, gz)
    theirs = pl.multiple_of(8 * (1 - gy), 8)
    mine = pl.multiple_of(8 * gy, 8)
    coarse_copy = pltpu.make_async_remote_copy(
        src_ref=coarse_ref.at[:, :, pl.ds(theirs, 8), :],
        dst_ref=pair_ref.at[gy],
        send_sem=send_b,
        recv_sem=recv_b,
        device_id=partner,
        device_id_type=MESH,
    )
    coarse_copy.start()
    copies = []
    for j in range(1, GROUP):
        copy = pltpu.make_async_remote_copy(
            src_ref=back_ref.at[mates[j - 1]],
            dst_ref=landed.at[m],
            send_sem=send_a.at[j - 1],
            recv_sem=recv_a.at[j - 1],
            device_id=mate_places[j - 1],
            device_id_type=MESH,
        )
        copy.start()
        copies.append(copy)
    landed[m] = back_ref[m]
    pair_ref[gy] = coarse_ref[:, :, pl.ds(mine, 8), :]
    for copy in copies:
        copy.wait()
    rows = swap_groups([landed[k].reshape(24, 128) for k in range(GROUP)])
    for x in range(8):
        v_ref[:, x] = rows[x].reshape(3, 8, 128)
    coarse_copy.wait()


def return_blocks(back, coarse):
    return pl.pallas_call(
        return_kernel,
        out_shape=(
            jax.ShapeDtypeStruct((3, 8, 8, 128), jnp.float32),
            jax.ShapeDtypeStruct((2, 3, 4, 8, 128), jnp.float32),
        ),
        in_specs=[VMEM_SPEC, VMEM_SPEC],
        out_specs=(VMEM_SPEC, VMEM_SPEC),
        scratch_shapes=[
            pltpu.VMEM((GROUP, 3, 8, 128), jnp.float32),
            pltpu.SemaphoreType.DMA((GROUP - 1,)),
            pltpu.SemaphoreType.DMA((GROUP - 1,)),
            pltpu.SemaphoreType.DMA,
            pltpu.SemaphoreType.DMA,
        ],
        compiler_params=pltpu.CompilerParams(
            collective_id=1, has_side_effects=True, vmem_limit_bytes=16 * 2**20
        ),
        name="return_blocks",
    )(back, coarse)


def total_kernel(count_z, sketch_ref, out_ref, part_ref, parts, sums, send_a, recv_a, send_b, recv_b, send_c, recv_c):
    gx, gy, gz = lax.axis_index("gx"), lax.axis_index("gy"), lax.axis_index("gz")
    m = 2 * gx + gy
    mates = [((m + j) % GROUP) for j in range(1, GROUP)]
    mate_places = [(k // 2, k % 2, gz) for k in mates]
    others = [((gz + j) % count_z) for j in range(1, count_z)]
    other_places = [(gx, gy, k) for k in others]
    greet(mate_places + other_places)
    part_ref[...] = gram_of(sketch_ref[...]).reshape(part_ref.shape)
    meet(mate_places + other_places)

    def send(src, dst, send_sem, recv_sem, place):
        copy = pltpu.make_async_remote_copy(
            src_ref=src, dst_ref=dst, send_sem=send_sem, recv_sem=recv_sem,
            device_id=place, device_id_type=MESH,
        )
        copy.start()
        return copy

    copies = [
        send(part_ref.at[mates[j]], parts.at[m], send_a.at[j], recv_a.at[j], mate_places[j])
        for j in range(GROUP - 1)
    ]
    parts[m] = part_ref[m]
    for copy in copies:
        copy.wait()
    total = parts[0]
    for k in range(1, GROUP):
        total = total + parts[k]
    sums[gz] = total
    copies = [
        send(sums.at[gz], sums.at[gz], send_b.at[j], recv_b.at[j], other_places[j])
        for j in range(count_z - 1)
    ]
    for copy in copies:
        copy.wait()
    total = sums[0]
    for k in range(1, count_z):
        total = total + sums[k]
    out_ref[m] = total
    copies = [
        send(out_ref.at[m], out_ref.at[m], send_c.at[j], recv_c.at[j], mate_places[j])
        for j in range(GROUP - 1)
    ]
    for copy in copies:
        copy.wait()


def total_over_devices(sketch_rows, count_z):
    rank = sketch_rows.shape[1]
    rows = rank // GROUP
    sems = pltpu.SemaphoreType.DMA
    out = pl.pallas_call(
        functools.partial(total_kernel, count_z),
        out_shape=jax.ShapeDtypeStruct((GROUP, rows, rank), jnp.float32),
        in_specs=[VMEM_SPEC],
        out_specs=VMEM_SPEC,
        scratch_shapes=[
            pltpu.VMEM((GROUP, rows, rank), jnp.float32),
            pltpu.VMEM((GROUP, rows, rank), jnp.float32),
            pltpu.VMEM((count_z, rows, rank), jnp.float32),
            sems((GROUP - 1,)),
            sems((GROUP - 1,)),
            sems((count_z - 1,)),
            sems((count_z - 1,)),
            sems((GROUP - 1,)),
            sems((GROUP - 1,)),
        ],
        compiler_params=pltpu.CompilerParams(collective_id=2, has_side_effects=True, vmem_limit_bytes=16 * 2**20),
        name="total_over_devices",
    )(sketch_rows)
    return out.reshape(rank, rank)


def omega_of(seed_matrix, snap_steps):
    picker = (
        snap_steps[:, None] == jnp.arange(seed_matrix.shape[0], dtype=jnp.int32)[None, :]
    ).astype(jnp.float32)
    return 0.5 * jnp.dot(picker, seed_matrix.astype(jnp.float32), precision=HIGHEST)


def factor_kernel(norm_scale, keep_ref, gram_ref, sketch_ref, rows_ref, factor_ref, unit):
    rank = gram_ref.shape[0]
    tiles = rank // 8
    down = lax.broadcasted_iota(jnp.int32, (8, rank), 0)
    lane = lax.broadcasted_iota(jnp.int32, (8, rank), 1)
    left = [gram_ref[8 * t : 8 * t + 8, :] for t in range(tiles)]
    right = [(lane == down + 8 * t).astype(jnp.float32) for t in range(tiles)]

    def spread(tile, i):
        return jnp.broadcast_to(tile[i : i + 1, :], (8, rank))

    for k in range(0, rank, 2):
        home, i = k // 8, k % 8
        first = [jnp.broadcast_to(left[t][:, k : k + 1], (8, rank)) for t in range(home, tiles)]
        second = [jnp.broadcast_to(left[t][:, k + 1 : k + 2], (8, rank)) for t in range(home, tiles)]
        p, q, s = spread(first[0], i), spread(second[0], i), spread(second[0], i + 1)
        inv_p = 1.0 / p
        ratio = q * inv_p
        inv_s = 1.0 / (s - ratio * q)
        row_a, row_za = spread(left[home], i), spread(right[home], i)
        row_b = spread(left[home], i + 1) - ratio * row_a
        row_zb = spread(right[home], i + 1) - ratio * row_za
        for t in range(home, tiles):
            m_a = first[t - home] * inv_p
            m_b = (second[t - home] - first[t - home] * ratio) * inv_s
            if t == home:
                m_a = jnp.where(down > i, m_a, 0.0)
                m_b = jnp.where(down > i + 1, m_b, 0.0)
            left[t] = left[t] - m_a * row_a - m_b * row_b
            right[t] = right[t] - m_a * row_za - m_b * row_zb
    keep = keep_ref[0]
    for t in range(tiles):
        at = down + 8 * t
        pivot = jnp.sum(jnp.where(lane == at, left[t], 0.0), axis=1, keepdims=True)
        scale = lax.rsqrt(pivot)
        inside = at < keep
        factor_ref[8 * t : 8 * t + 8, :] = jnp.where(
            inside & (lane < keep) & (lane >= at), left[t] * (scale * (1.0 / norm_scale)), 0.0
        )
        unit[8 * t : 8 * t + 8, :] = jnp.where(inside, right[t] * (scale * norm_scale), 0.0)
    rows_ref[...] = lax.dot_general(
        sketch_ref[...], unit[...], (((1,), (1,)), ((), ())),
        precision=HIGHEST, preferred_element_type=jnp.float32,
    )


def finish(sketch_rows, gram_sum, rank_keep, shape):
    rank = shape[-1]
    total_rows = (
        sketch_rows.shape[0] * lax.axis_size("gx") * lax.axis_size("gy") * lax.axis_size("gz")
    )
    mode_rows, factor = pl.pallas_call(
        functools.partial(factor_kernel, math.sqrt(total_rows)),
        out_shape=(
            jax.ShapeDtypeStruct(sketch_rows.shape, jnp.float32),
            jax.ShapeDtypeStruct((rank, rank), jnp.float32),
        ),
        in_specs=[pl.BlockSpec(memory_space=pltpu.SMEM), VMEM_SPEC, VMEM_SPEC],
        out_specs=(VMEM_SPEC, VMEM_SPEC),
        scratch_shapes=[pltpu.VMEM((rank, rank), jnp.float32)],
        compiler_params=pltpu.CompilerParams(vmem_limit_bytes=24 * 2**20),
        name="factor_and_rows",
    )(rank_keep, gram_sum, sketch_rows)
    return mode_rows.reshape(shape), factor


def gram_of(sketch_rows):
    return lax.dot_general(
        sketch_rows, sketch_rows, (((0,), (0,)), ((), ())), precision=HIGHEST
    )


def by_chunks(velocity, sketch_prev, seed_matrix, snap_steps, rank_keep):
    rank_total = sketch_prev.shape[-1]
    count_z = lax.axis_size("gz")
    ext = gather_blocks(velocity, GROUP * count_z)
    back, coarse = solve_window(ext)
    current, pair = return_blocks(back, coarse)
    omega = omega_of(seed_matrix, snap_steps)
    spread = pair.reshape(2, 3, 4, 8, 2, 64)[..., HALO : HALO + CHUNK].reshape(2, 3, 4, 8, 2, 4, 4)
    snap_rows = jnp.transpose(spread, (6, 1, 3, 0, 5, 4, 2)).reshape(SNAPS, -1)
    sketch_rows = sketch_prev.reshape(-1, rank_total) + lax.dot_general(
        snap_rows, omega, (((0,), (0,)), ((), ())), precision=HIGHEST
    )
    gram_sum = total_over_devices(sketch_rows, count_z)
    return (current,) + finish(sketch_rows, gram_sum, rank_keep, sketch_prev.shape)


def step_by_step(velocity, sketch_prev, seed_matrix, snap_steps, rank_keep):
    current = velocity
    collected = []
    for snap_index in range(SNAPS):
        for step_index in range(STEPS):
            current = step_by_section(current)
        local_snap = coarse_local(current)
        collected.append(lax.all_to_all(local_snap, "gx", split_axis=2, concat_axis=3, tiled=True))
    stacked = jnp.stack(collected)
    rank_total = sketch_prev.shape[-1]
    snap_rows = stacked.reshape(stacked.shape[0], -1)
    omega_rows = omega_of(seed_matrix, snap_steps)
    sketch_rows = sketch_prev.reshape(-1, rank_total) + lax.dot_general(
        snap_rows, omega_rows, (((0,), (0,)), ((), ())), precision=HIGHEST
    )
    gram_sum = lax.psum(gram_of(sketch_rows), ("gx", "gy", "gz"))
    return (current,) + finish(sketch_rows, gram_sum, rank_keep, sketch_prev.shape)


def on_device(velocity, sketch_prev, seed_matrix, snap_steps, rank_keep):
    fits = (
        (lax.axis_size("gx"), lax.axis_size("gy")) == (4, 2)
        and lax.axis_size("gz") >= 2
        and velocity.shape == (3, 8, 8, 128)
        and sketch_prev.shape == (3, 8, 1, 8, 8, 128)
    )
    run = by_chunks if fits else step_by_step
    return run(velocity, sketch_prev, seed_matrix, snap_steps, rank_keep)


def solution(mesh):
    placed = (P(None, "gx", "gy", "gz"), P(None, "gy", "gz", "gx", None, None), P(), P(), P())
    return jax.shard_map(
        on_device,
        mesh=mesh,
        in_specs=placed,
        out_specs=(P(None, "gx", "gy", "gz"), P(None, "gy", "gz", "gx", None, None), P()),
        check_vma=False,
    )
```

```python
import functools
import math

import jax
import jax.numpy as jnp
from jax import lax
from jax.experimental import pallas as pl
from jax.experimental.pallas import tpu as pltpu
from jax.sharding import PartitionSpec as P

MESH = pl.DeviceIdType.MESH
VMEM_SPEC = pl.BlockSpec(memory_space=pltpu.VMEM)

SNAPS = 4
STEPS = 2


TIME_STEP = 0.1
VISCOSITY = 0.4
ONE_THIRD = 1.0 / 3.0
TWO_THIRDS = 2.0 / 3.0
HIGHEST = lax.Precision.HIGHEST


def extended(block, sides, width):
    for axis, dim in sides:
        count = lax.axis_size(axis)
        forward = [(i, i + 1) for i in range(count - 1)]
        forward.append((count - 1, 0))
        backward = [(target, source) for source, target in forward]
        low = lax.ppermute(
            lax.slice_in_dim(block, block.shape[dim] - width, None, axis=dim), axis, forward
        )
        high = lax.ppermute(lax.slice_in_dim(block, 0, width, axis=dim), axis, backward)
        block = jnp.concatenate([low, block, high], axis=dim)
    return block


def tendency(padded):
    center = padded[:, 1:-1, 1:-1, 1:-1]
    forward = (padded[:, 2:, 1:-1, 1:-1], padded[:, 1:-1, 2:, 1:-1], padded[:, 1:-1, 1:-1, 2:])
    backward = (padded[:, :-2, 1:-1, 1:-1], padded[:, 1:-1, :-2, 1:-1], padded[:, 1:-1, 1:-1, :-2])
    convect = (
        center[0:1] * (forward[0] - backward[0])
        + center[1:2] * (forward[1] - backward[1])
        + center[2:3] * (forward[2] - backward[2])
    )
    spread = (
        forward[0]
        + backward[0]
        + forward[1]
        + backward[1]
        + forward[2]
        + backward[2]
        - 6.0 * center
    )
    return -0.5 * convect + VISCOSITY * spread


def with_walls(padded, margin):
    cells_y = padded.shape[2] - 2 * margin
    wall_rows = (
        lax.axis_index("gy") * cells_y - margin + jnp.arange(cells_y + 2 * margin, dtype=jnp.int32)
    )
    inside = ((wall_rows >= 0) & (wall_rows < lax.axis_size("gy") * cells_y)).astype(jnp.float32)
    return padded * inside[None, None, :, None]


def faces_padded(current):
    return with_walls(extended(current, (("gx", 1), ("gy", 2), ("gz", 3)), 1), 1)


def step_by_section(current):
    first_section = current + TIME_STEP * tendency(faces_padded(current))
    second_section = 0.75 * current + 0.25 * (
        first_section + TIME_STEP * tendency(faces_padded(first_section))
    )
    return ONE_THIRD * current + TWO_THIRDS * (
        second_section + TIME_STEP * tendency(faces_padded(second_section))
    )


def coarse_local(current):
    cells_x = current.shape[1]
    cells_y = current.shape[2]
    cells_z = current.shape[3]
    blocks = current.reshape(3, cells_x // 4, 4, cells_y, cells_z // 4, 4)
    return jnp.transpose(jnp.mean(blocks, axis=(2, 5)), (0, 2, 3, 1))


GROUP = 8
CHUNK = 16
HALO = 24
REACH = (-2, -1, 0, 1, 2)


def place_of(n):
    m = n % GROUP
    return (m // 2, m % 2, n // GROUP)


def swap_groups(rows):
    rows = list(rows)
    lane = lax.broadcasted_iota(jnp.int32, rows[0].shape, 1)
    for step in (1, 2, 4):
        low = (lane // (CHUNK * step)) % 2 == 0
        for i in range(GROUP):
            if i & step:
                continue
            first, second = rows[i], rows[i | step]
            rows[i] = jnp.where(low, first, pltpu.roll(second, CHUNK * step, 1))
            rows[i | step] = jnp.where(low, pltpu.roll(first, 128 - CHUNK * step, 1), second)
    return rows


def greet(places):
    barrier = pltpu.get_barrier_semaphore()
    for place in places:
        pl.semaphore_signal(barrier, inc=1, device_id=place, device_id_type=MESH)


def meet(places):
    pl.semaphore_wait(pltpu.get_barrier_semaphore(), len(places))


def gather_kernel(ring, v_ref, ext_ref, packed, send_a, recv_a, send_b, recv_b):
    gx, gy, gz = lax.axis_index("gx"), lax.axis_index("gy"), lax.axis_index("gz")
    m = 2 * gx + gy
    n = GROUP * gz + m
    mates = [((m + j) % GROUP) for j in range(1, GROUP)]
    mate_places = [(k // 2, k % 2, gz) for k in mates]
    offsets = [d for d in REACH if d != 0]
    ring_places = [place_of((n + d + ring) % ring) for d in offsets]
    greet(mate_places + ring_places)
    rows = swap_groups([v_ref[:, x].reshape(24, 128) for x in range(8)])
    for k in range(GROUP):
        packed[k] = rows[k].reshape(3, 8, 128)
    meet(mate_places + ring_places)
    copies = []
    for j in range(1, GROUP):
        copy = pltpu.make_async_remote_copy(
            src_ref=packed.at[mates[j - 1]],
            dst_ref=ext_ref.at[2, m],
            send_sem=send_a.at[j - 1],
            recv_sem=recv_a.at[j - 1],
            device_id=mate_places[j - 1],
            device_id_type=MESH,
        )
        copy.start()
        copies.append(copy)
    ext_ref[2, m] = packed[m]
    for copy in copies:
        copy.wait()
    copies = []
    for i, d in enumerate(offsets):
        copy = pltpu.make_async_remote_copy(
            src_ref=ext_ref.at[2],
            dst_ref=ext_ref.at[2 - d],
            send_sem=send_b.at[i],
            recv_sem=recv_b.at[i],
            device_id=ring_places[i],
            device_id_type=MESH,
        )
        copy.start()
        copies.append(copy)
    for copy in copies:
        copy.wait()


def gather_blocks(velocity, ring):
    return pl.pallas_call(
        functools.partial(gather_kernel, ring),
        out_shape=jax.ShapeDtypeStruct((5, GROUP, 3, 8, 128), jnp.float32),
        in_specs=[VMEM_SPEC],
        out_specs=VMEM_SPEC,
        scratch_shapes=[
            pltpu.VMEM((GROUP, 3, 8, 128), jnp.float32),
            pltpu.SemaphoreType.DMA((GROUP - 1,)),
            pltpu.SemaphoreType.DMA((GROUP - 1,)),
            pltpu.SemaphoreType.DMA((4,)),
            pltpu.SemaphoreType.DMA((4,)),
        ],
        compiler_params=pltpu.CompilerParams(
            collective_id=0, has_side_effects=True, vmem_limit_bytes=16 * 2**20
        ),
        name="gather_blocks",
    )(velocity)


def wrap_rows(buf):
    buf[:, 0] = pltpu.roll(buf[:, 16].reshape(48, 128), 64, 1).reshape(3, 16, 128)
    buf[:, 17] = pltpu.roll(buf[:, 1].reshape(48, 128), 64, 1).reshape(3, 16, 128)


def section(src, base, dst, base_weight, weight):
    row = lax.broadcasted_iota(jnp.int32, (16, 128), 0)
    top, bottom = row == 15, row == 0
    even = weight * TIME_STEP * VISCOSITY
    odd = weight * TIME_STEP * 0.5
    own = weight * (1.0 - 6.0 * TIME_STEP * VISCOSITY)

    def one_row(r, carry):
        center = [src[c, r] for c in range(3)]
        ahead = [even - odd * center[j] for j in range(3)]
        behind = [2.0 * even - ahead[j] for j in range(3)]
        ahead[1] = jnp.where(top, 0.0, ahead[1])
        behind[1] = jnp.where(bottom, 0.0, behind[1])
        for c in range(3):
            value = own * center[c]
            x_part = ahead[0] * src[c, r + 1] + behind[0] * src[c, r - 1]
            y_part = ahead[1] * pltpu.roll(center[c], 15, 0) + behind[1] * pltpu.roll(center[c], 1, 0)
            z_part = ahead[2] * pltpu.roll(center[c], 127, 1) + behind[2] * pltpu.roll(center[c], 1, 1)
            if base is not None:
                value = value + base_weight * base[c, r]
            dst[c, r] = (value + x_part) + (y_part + z_part)
        return carry

    for r in range(1, 17):
        one_row(r, 0)
    wrap_rows(dst)


def solve_kernel(ext_ref, back_ref, coarse_ref, v, a, b):
    lane = lax.broadcasted_iota(jnp.int32, (24, 128), 1)
    for far in range(2):
        for y_half in range(2):
            for x in range(8):
                value = None
                for half in range(2):
                    for d in REACH:
                        piece = ext_ref[d + 2, 2 * (2 * half + far) + y_half].reshape(24, 128)
                        start = 64 * half + HALO + CHUNK * d
                        piece = pltpu.roll(piece, (start - CHUNK * x) % 128, 1)
                        if value is None:
                            value = piece
                        else:
                            first = max(start, 64 * half)
                            value = jnp.where(lane >= first, piece, value)
                v[:, 1 + 8 * far + x, 8 * y_half : 8 * y_half + 8, :] = value.reshape(3, 8, 128)
    wrap_rows(v)
    wide = lax.broadcasted_iota(jnp.int32, (16, 128), 1)

    def one_step(step, carry):
        section(v, None, a, 0.0, 1.0)
        section(a, v, b, 0.75, 0.25)
        section(b, v, v, ONE_THIRD, TWO_THIRDS)
        return carry

    coarse_ref[...] = jnp.zeros(coarse_ref.shape, jnp.float32)

    def one_snap(k, carry):
        lax.fori_loop(0, STEPS, one_step, 0)
        for c in range(3):
            for block in range(4):
                at = 1 + 4 * block
                total = (v[c, at] + v[c, at + 1]) + (v[c, at + 2] + v[c, at + 3])
                total = total + pltpu.roll(total, 127, 1)
                total = total + pltpu.roll(total, 126, 1)
                total = pltpu.roll(total * (1.0 / 16.0), k, 1)
                coarse_ref[c, block] = jnp.where(wide % 4 == k, total, coarse_ref[c, block])
        return carry

    lax.fori_loop(0, SNAPS, one_snap, 0)
    group = lax.broadcasted_iota(jnp.int32, (24, 128), 1) // CHUNK
    for half in range(2):
        for far in range(2):
            for y_half in range(2):
                value = None
                for x in range(8):
                    piece = v[:, 1 + 8 * far + x, 8 * y_half : 8 * y_half + 8, :].reshape(24, 128)
                    piece = pltpu.roll(piece, (CHUNK * x - 64 * half - HALO) % 128, 1)
                    value = piece if value is None else jnp.where(group >= x, piece, value)
                back_ref[2 * (2 * half + far) + y_half] = value.reshape(3, 8, 128)


def solve_window(ext):
    field = pltpu.VMEM((3, 18, 16, 128), jnp.float32)
    return pl.pallas_call(
        solve_kernel,
        out_shape=(
            jax.ShapeDtypeStruct((GROUP, 3, 8, 128), jnp.float32),
            jax.ShapeDtypeStruct((3, 4, 16, 128), jnp.float32),
        ),
        in_specs=[VMEM_SPEC],
        out_specs=(VMEM_SPEC, VMEM_SPEC),
        scratch_shapes=[field, field, field],
        compiler_params=pltpu.CompilerParams(vmem_limit_bytes=24 * 2**20),
        name="solve_window",
    )(ext)


def return_kernel(back_ref, coarse_ref, v_ref, pair_ref, landed, send_a, recv_a, send_b, recv_b):
    gx, gy, gz = lax.axis_index("gx"), lax.axis_index("gy"), lax.axis_index("gz")
    m = 2 * gx + gy
    mates = [((m + j) % GROUP) for j in range(1, GROUP)]
    mate_places = [(k // 2, k % 2, gz) for k in mates]
    greet(mate_places)
    meet(mate_places)
    partner = (gx, 1 - gy, gz)
    theirs = pl.multiple_of(8 * (1 - gy), 8)
    mine = pl.multiple_of(8 * gy, 8)
    coarse_copy = pltpu.make_async_remote_copy(
        src_ref=coarse_ref.at[:, :, pl.ds(theirs, 8), :],
        dst_ref=pair_ref.at[gy],
        send_sem=send_b,
        recv_sem=recv_b,
        device_id=partner,
        device_id_type=MESH,
    )
    coarse_copy.start()
    copies = []
    for j in range(1, GROUP):
        copy = pltpu.make_async_remote_copy(
            src_ref=back_ref.at[mates[j - 1]],
            dst_ref=landed.at[m],
            send_sem=send_a.at[j - 1],
            recv_sem=recv_a.at[j - 1],
            device_id=mate_places[j - 1],
            device_id_type=MESH,
        )
        copy.start()
        copies.append(copy)
    landed[m] = back_ref[m]
    pair_ref[gy] = coarse_ref[:, :, pl.ds(mine, 8), :]
    for copy in copies:
        copy.wait()
    rows = swap_groups([landed[k].reshape(24, 128) for k in range(GROUP)])
    for x in range(8):
        v_ref[:, x] = rows[x].reshape(3, 8, 128)
    coarse_copy.wait()


def return_blocks(back, coarse):
    return pl.pallas_call(
        return_kernel,
        out_shape=(
            jax.ShapeDtypeStruct((3, 8, 8, 128), jnp.float32),
            jax.ShapeDtypeStruct((2, 3, 4, 8, 128), jnp.float32),
        ),
        in_specs=[VMEM_SPEC, VMEM_SPEC],
        out_specs=(VMEM_SPEC, VMEM_SPEC),
        scratch_shapes=[
            pltpu.VMEM((GROUP, 3, 8, 128), jnp.float32),
            pltpu.SemaphoreType.DMA((GROUP - 1,)),
            pltpu.SemaphoreType.DMA((GROUP - 1,)),
            pltpu.SemaphoreType.DMA,
            pltpu.SemaphoreType.DMA,
        ],
        compiler_params=pltpu.CompilerParams(
            collective_id=1, has_side_effects=True, vmem_limit_bytes=16 * 2**20
        ),
        name="return_blocks",
    )(back, coarse)


def total_kernel(count_z, sketch_ref, out_ref, part_ref, parts, sums, send_a, recv_a, send_b, recv_b, send_c, recv_c):
    gx, gy, gz = lax.axis_index("gx"), lax.axis_index("gy"), lax.axis_index("gz")
    m = 2 * gx + gy
    mates = [((m + j) % GROUP) for j in range(1, GROUP)]
    mate_places = [(k // 2, k % 2, gz) for k in mates]
    others = [((gz + j) % count_z) for j in range(1, count_z)]
    other_places = [(gx, gy, k) for k in others]
    greet(mate_places + other_places)
    part_ref[...] = gram_of(sketch_ref[...]).reshape(part_ref.shape)
    meet(mate_places + other_places)

    def send(src, dst, send_sem, recv_sem, place):
        copy = pltpu.make_async_remote_copy(
            src_ref=src, dst_ref=dst, send_sem=send_sem, recv_sem=recv_sem,
            device_id=place, device_id_type=MESH,
        )
        copy.start()
        return copy

    copies = [
        send(part_ref.at[mates[j]], parts.at[m], send_a.at[j], recv_a.at[j], mate_places[j])
        for j in range(GROUP - 1)
    ]
    parts[m] = part_ref[m]
    for copy in copies:
        copy.wait()
    total = parts[0]
    for k in range(1, GROUP):
        total = total + parts[k]
    sums[gz] = total
    copies = [
        send(sums.at[gz], sums.at[gz], send_b.at[j], recv_b.at[j], other_places[j])
        for j in range(count_z - 1)
    ]
    for copy in copies:
        copy.wait()
    total = sums[0]
    for k in range(1, count_z):
        total = total + sums[k]
    out_ref[m] = total
    copies = [
        send(out_ref.at[m], out_ref.at[m], send_c.at[j], recv_c.at[j], mate_places[j])
        for j in range(GROUP - 1)
    ]
    for copy in copies:
        copy.wait()


def total_over_devices(sketch_rows, count_z):
    rank = sketch_rows.shape[1]
    rows = rank // GROUP
    sems = pltpu.SemaphoreType.DMA
    out = pl.pallas_call(
        functools.partial(total_kernel, count_z),
        out_shape=jax.ShapeDtypeStruct((GROUP, rows, rank), jnp.float32),
        in_specs=[VMEM_SPEC],
        out_specs=VMEM_SPEC,
        scratch_shapes=[
            pltpu.VMEM((GROUP, rows, rank), jnp.float32),
            pltpu.VMEM((GROUP, rows, rank), jnp.float32),
            pltpu.VMEM((count_z, rows, rank), jnp.float32),
            sems((GROUP - 1,)),
            sems((GROUP - 1,)),
            sems((count_z - 1,)),
            sems((count_z - 1,)),
            sems((GROUP - 1,)),
            sems((GROUP - 1,)),
        ],
        compiler_params=pltpu.CompilerParams(collective_id=2, has_side_effects=True, vmem_limit_bytes=16 * 2**20),
        name="total_over_devices",
    )(sketch_rows)
    return out.reshape(rank, rank)


def omega_of(seed_matrix, snap_steps):
    picker = (
        snap_steps[:, None] == jnp.arange(seed_matrix.shape[0], dtype=jnp.int32)[None, :]
    ).astype(jnp.float32)
    return 0.5 * jnp.dot(picker, seed_matrix.astype(jnp.float32), precision=HIGHEST)


def factor_kernel(norm_scale, keep_ref, gram_ref, sketch_ref, rows_ref, factor_ref, unit):
    rank = gram_ref.shape[0]
    tiles = rank // 8
    down = lax.broadcasted_iota(jnp.int32, (8, rank), 0)
    lane = lax.broadcasted_iota(jnp.int32, (8, rank), 1)
    left = [gram_ref[8 * t : 8 * t + 8, :] for t in range(tiles)]
    right = [(lane == down + 8 * t).astype(jnp.float32) for t in range(tiles)]

    def spread(tile, i):
        return jnp.broadcast_to(tile[i : i + 1, :], (8, rank))

    for k in range(0, rank, 2):
        home, i = k // 8, k % 8
        first = [jnp.broadcast_to(left[t][:, k : k + 1], (8, rank)) for t in range(home, tiles)]
        second = [jnp.broadcast_to(left[t][:, k + 1 : k + 2], (8, rank)) for t in range(home, tiles)]
        p, q, s = spread(first[0], i), spread(second[0], i), spread(second[0], i + 1)
        inv_p = 1.0 / p
        ratio = q * inv_p
        inv_s = 1.0 / (s - ratio * q)
        row_a, row_za = spread(left[home], i), spread(right[home], i)
        row_b = spread(left[home], i + 1) - ratio * row_a
        row_zb = spread(right[home], i + 1) - ratio * row_za
        for t in range(home, tiles):
            m_a = first[t - home] * inv_p
            m_b = (second[t - home] - first[t - home] * ratio) * inv_s
            if t == home:
                m_a = jnp.where(down > i, m_a, 0.0)
                m_b = jnp.where(down > i + 1, m_b, 0.0)
            left[t] = left[t] - m_a * row_a - m_b * row_b
            right[t] = right[t] - m_a * row_za - m_b * row_zb
    keep = keep_ref[0]
    for t in range(tiles):
        at = down + 8 * t
        pivot = jnp.sum(jnp.where(lane == at, left[t], 0.0), axis=1, keepdims=True)
        scale = lax.rsqrt(pivot)
        inside = at < keep
        factor_ref[8 * t : 8 * t + 8, :] = jnp.where(
            inside & (lane < keep) & (lane >= at), left[t] * (scale * (1.0 / norm_scale)), 0.0
        )
        unit[8 * t : 8 * t + 8, :] = jnp.where(inside, right[t] * (scale * norm_scale), 0.0)
    rows_ref[...] = lax.dot_general(
        sketch_ref[...], unit[...], (((1,), (1,)), ((), ())),
        precision=HIGHEST, preferred_element_type=jnp.float32,
    )


def finish(sketch_rows, gram_sum, rank_keep, shape):
    rank = shape[-1]
    total_rows = (
        sketch_rows.shape[0] * lax.axis_size("gx") * lax.axis_size("gy") * lax.axis_size("gz")
    )
    mode_rows, factor = pl.pallas_call(
        functools.partial(factor_kernel, math.sqrt(total_rows)),
        out_shape=(
            jax.ShapeDtypeStruct(sketch_rows.shape, jnp.float32),
            jax.ShapeDtypeStruct((rank, rank), jnp.float32),
        ),
        in_specs=[pl.BlockSpec(memory_space=pltpu.SMEM), VMEM_SPEC, VMEM_SPEC],
        out_specs=(VMEM_SPEC, VMEM_SPEC),
        scratch_shapes=[pltpu.VMEM((rank, rank), jnp.float32)],
        compiler_params=pltpu.CompilerParams(vmem_limit_bytes=24 * 2**20),
        name="factor_and_rows",
    )(rank_keep, gram_sum, sketch_rows)
    return mode_rows.reshape(shape), factor


def gram_of(sketch_rows):
    return lax.dot_general(
        sketch_rows, sketch_rows, (((0,), (0,)), ((), ())), precision=HIGHEST
    )


def by_chunks(velocity, sketch_prev, seed_matrix, snap_steps, rank_keep):
    rank_total = sketch_prev.shape[-1]
    count_z = lax.axis_size("gz")
    ext = gather_blocks(velocity, GROUP * count_z)
    back, coarse = solve_window(ext)
    current, pair = return_blocks(back, coarse)
    omega = omega_of(seed_matrix, snap_steps)
    spread = pair.reshape(2, 3, 4, 8, 2, 64)[..., HALO : HALO + CHUNK].reshape(2, 3, 4, 8, 2, 4, 4)
    snap_rows = jnp.transpose(spread, (6, 1, 3, 0, 5, 4, 2)).reshape(SNAPS, -1)
    sketch_rows = sketch_prev.reshape(-1, rank_total) + lax.dot_general(
        snap_rows, omega, (((0,), (0,)), ((), ())), precision=HIGHEST
    )
    gram_sum = total_over_devices(sketch_rows, count_z)
    return (current,) + finish(sketch_rows, gram_sum, rank_keep, sketch_prev.shape)


def step_by_step(velocity, sketch_prev, seed_matrix, snap_steps, rank_keep):
    current = velocity
    collected = []
    for snap_index in range(SNAPS):
        for step_index in range(STEPS):
            current = step_by_section(current)
        local_snap = coarse_local(current)
        collected.append(lax.all_to_all(local_snap, "gx", split_axis=2, concat_axis=3, tiled=True))
    stacked = jnp.stack(collected)
    rank_total = sketch_prev.shape[-1]
    snap_rows = stacked.reshape(stacked.shape[0], -1)
    omega_rows = omega_of(seed_matrix, snap_steps)
    sketch_rows = sketch_prev.reshape(-1, rank_total) + lax.dot_general(
        snap_rows, omega_rows, (((0,), (0,)), ((), ())), precision=HIGHEST
    )
    gram_sum = lax.psum(gram_of(sketch_rows), ("gx", "gy", "gz"))
    return (current,) + finish(sketch_rows, gram_sum, rank_keep, sketch_prev.shape)


def on_device(velocity, sketch_prev, seed_matrix, snap_steps, rank_keep):
    fits = (
        (lax.axis_size("gx"), lax.axis_size("gy")) == (4, 2)
        and lax.axis_size("gz") >= 2
        and velocity.shape == (3, 8, 8, 128)
        and sketch_prev.shape == (3, 8, 1, 8, 8, 128)
    )
    run = by_chunks if fits else step_by_step
    return run(velocity, sketch_prev, seed_matrix, snap_steps, rank_keep)


def solution(mesh):
    placed = (P(None, "gx", "gy", "gz"), P(None, "gy", "gz", "gx", None, None), P(), P(), P())
    return jax.shard_map(
        on_device,
        mesh=mesh,
        in_specs=placed,
        out_specs=(P(None, "gx", "gy", "gz"), P(None, "gy", "gz", "gx", None, None), P()),
        check_vma=False,
    )
```
